32 devices in a mesh: section: 4 (over z), row: 2 (over x), col: 4 (over y, core).
Axes of the slice: x: 2, y: 2, z: 4, core: 2. Of those that a mesh axis runs over, the one named last changes fastest.
Arguments:
- tokens: bfloat16 [4, 512, 4096], P('section', 'col', 'row'), may hold values from -6 to 6
- cotangent: bfloat16 [4, 512, 4096], P('section', 'col', 'row'), may hold values from -6 to 6
- noised: int32 [4, 512], P('section', 'col'), may hold values from 0 to 1, as said below
- gate_weight: bfloat16 [4, 4096, 16384], P('section', None, ('row', 'col')), may hold values from -0.09375 to 0.09375
- up_weight: bfloat16 [4, 4096, 16384], P('section', None, ('row', 'col')), may hold values from -0.09375 to 0.09375
- down_weight: bfloat16 [4, 16384, 4096], P('section', ('row', 'col')), may hold values from -0.046875 to 0.046875
- block_keep: int32 [4, 3, 32, 128], P('section', None, None, ('row', 'col')), may hold values 0 or 1
Outputs:
- grad_gate: bfloat16 [4, 4096, 16384], P('section', None, ('row', 'col'))
- grad_up: bfloat16 [4, 4096, 16384], P('section', None, ('row', 'col'))
- grad_down: bfloat16 [4, 16384, 4096], P('section', ('row', 'col'))
- handoff: bfloat16 [4, 512, 4096], P('section', 'col')
The draws below stay inside these ranges and needn't reach their ends.
Inputs may be any that keep to these rules, and one draw needn't show every extreme that they name: Each aligned block of 128 tokens of a section (the tokens of one grid column) holds 1 to 96 noised tokens; in every section some block holds exactly 96.
All inputs are finite; a program needn't handle non-finite values. No bound on the sum of `block_keep` on one device may be relied on, other than what follows from the above.
Results may differ from the reference program's by a relative error of at most 0.0051.
Values may be sent and summed in bfloat16 or wider, within the bound.
A program may use at most 256 MiB of HBM per device.

```python
import jax
import jax.numpy as jnp
from jax import lax

D = 4096
FF = 16384
TOK_DEV = 128
CAP = 96
TOKENS = 512
N_SECTION = 4


def draw_noised(key, part):
    blocks_count = TOKENS // TOK_DEV
    sections_count = N_SECTION
    base = jax.random.fold_in(key, 17)
    first_key, second_key, third_key = jax.random.split(base, 3)
    counts = jax.random.randint(first_key, (sections_count, blocks_count), 1, CAP + 1)
    fullest = jax.random.randint(second_key, (sections_count, 1), 0, blocks_count)
    counts = jnp.where(jnp.arange(blocks_count)[None, :] == fullest, CAP, counts)
    block_keys = jax.random.split(third_key, sections_count * blocks_count)
    ranking = jax.vmap(lambda single: jax.random.permutation(single, TOK_DEV))(block_keys)
    ranking = ranking.reshape(sections_count, blocks_count, TOK_DEV)
    chosen = (ranking < counts[:, :, None]).astype(jnp.int32)
    return chosen.reshape(sections_count, TOKENS)


def set_ends(result, stream_key, least, high):
    shape = result.shape
    spot = [jax.random.randint(jax.random.fold_in(stream_key, axis), (), 0, shape[axis]) for axis in range(len(shape))]
    result = result.at[tuple(spot)].set(least)
    longest = shape.index(max(shape))
    spot[longest] = (spot[longest] + 1) % shape[longest]
    return result.at[tuple(spot)].set(high)


def level_of(stream_key, extent, shards, smallest, largest):
    level = 1.0
    for dim, shards_of in shards:
        steps = jax.random.uniform(jax.random.fold_in(jax.random.fold_in(stream_key, 6), dim), (shards_of,), jnp.float32, smallest / len(shards), largest / len(shards))
        level = level * jnp.repeat(jnp.exp(steps), extent[dim] // shards_of).reshape((-1,) + (1,) * (len(extent) - 1 - dim))
    return level


def centred(stream_key, shape, spread, most, cuts=(), held_as=jnp.bfloat16):
    drawn = spread * jax.random.normal(stream_key, shape, jnp.float32)
    if cuts:
        drawn = drawn * level_of(stream_key, shape, cuts, -0.22, 0.18)
    return jnp.clip(drawn, -most, most).astype(held_as)


def setup_inputs(seed: int = 0) -> dict:
    streams_of = jax.random.split(jax.random.key(seed), 8)
    return {
        "tokens": centred(streams_of[0], (N_SECTION, TOKENS, D), 1.0, 6.0, ((0, 4), (1, 4), (2, 2))),
        "cotangent": centred(streams_of[1], (N_SECTION, TOKENS, D), 1.0, 6.0, ((0, 4), (1, 4), (2, 2))),
        "noised": draw_noised(jax.random.fold_in(streams_of[7], 71), 0),
        "gate_weight": centred(streams_of[3], (N_SECTION, D, FF), D ** -0.5, 0.09375, ((0, 4), (2, 8))),
        "up_weight": centred(streams_of[4], (N_SECTION, D, FF), D ** -0.5, 0.09375, ((0, 4), (2, 8))),
        "down_weight": centred(streams_of[5], (N_SECTION, FF, D), FF ** -0.5, 0.046875, ((0, 4), (1, 8))),
        "block_keep": set_ends((jax.random.randint(streams_of[6], (N_SECTION, 3, D // 128, FF // 128), 0, 2) < 1).astype(jnp.int32), jax.random.fold_in(streams_of[6], 1), 0, 1),
    }


def expand_blocks(block_mask, block_edge):
    widened = jnp.repeat(jnp.repeat(block_mask, block_edge, axis=0), block_edge, axis=1)
    return widened.astype(jnp.bfloat16)


def contract_rows(left, right):
    return lax.dot_general(left, right, (((0,), (0,)), ((), ())), preferred_element_type=jnp.float32)


def contract_cols(left, right):
    return lax.dot_general(left, right, (((1,), (1,)), ((), ())), preferred_element_type=jnp.float32)


def layer_grads(tokens, cotangent, noised, gate_weight, up_weight, down_weight, block_keep):
    gate_mask = expand_blocks(block_keep[0], 128)
    up_mask = expand_blocks(block_keep[1], 128)
    down_mask = expand_blocks(block_keep[2].T, 128)
    gate_eff = gate_weight * gate_mask
    up_eff = up_weight * up_mask
    down_eff = down_weight * down_mask
    masked_cot = cotangent * noised[:, None].astype(jnp.bfloat16)
    gate_pre = jnp.dot(tokens, gate_eff, preferred_element_type=jnp.float32)
    up_pre = jnp.dot(tokens, up_eff, preferred_element_type=jnp.float32)
    sigmoid_gate = jax.nn.sigmoid(gate_pre)
    silu_gate = gate_pre * sigmoid_gate
    hidden = (silu_gate * up_pre).astype(jnp.bfloat16)
    grad_hidden = contract_cols(masked_cot, down_eff)
    grad_down = (contract_rows(hidden, masked_cot) * down_mask).astype(jnp.bfloat16)
    grad_gate_pre = (grad_hidden * up_pre * sigmoid_gate * (1.0 + gate_pre * (1.0 - sigmoid_gate))).astype(jnp.bfloat16)
    grad_up_pre = (grad_hidden * silu_gate).astype(jnp.bfloat16)
    grad_gate = (contract_rows(tokens, grad_gate_pre) * gate_mask).astype(jnp.bfloat16)
    grad_up = (contract_rows(tokens, grad_up_pre) * up_mask).astype(jnp.bfloat16)
    grad_input = (contract_cols(grad_gate_pre, gate_eff) + contract_cols(grad_up_pre, up_eff)).astype(jnp.bfloat16)
    return grad_gate, grad_up, grad_down, grad_input


def reference(tokens, cotangent, noised, gate_weight, up_weight, down_weight, block_keep):
    results = []
    for section_index in range(tokens.shape[0]):
        results.append(layer_grads(tokens[section_index], cotangent[section_index], noised[section_index],
                                   gate_weight[section_index], up_weight[section_index],
                                   down_weight[section_index], block_keep[section_index]))
    grad_gate = jnp.stack([entry[0] for entry in results])
    grad_up = jnp.stack([entry[1] for entry in results])
    grad_down = jnp.stack([entry[2] for entry in results])
    inputs_grad = jnp.stack([entry[3] for entry in results])
    handoff = jnp.concatenate([inputs_grad[1:], jnp.zeros_like(inputs_grad[:1])], axis=0)
    return grad_gate, grad_up, grad_down, handoff
```

```python
import jax
import jax.numpy as jnp
from jax import lax
from jax.experimental import pallas as pl
from jax.experimental.pallas import tpu as pltpu
from jax.sharding import PartitionSpec as P

CAP = 96
EDGE = 128
SUB = 16
VMEM = 44 * 1024 * 1024


def dot(left, right, left_dim, right_dim):
    return lax.dot_general(
        left,
        right,
        (((left_dim,), (right_dim,)), ((), ())),
        preferred_element_type=jnp.float32,
    )


def masked(values, mask):
    blocks, _, cols = mask.shape
    split = values.reshape(blocks, EDGE // SUB, SUB, cols)
    return (split * mask[:, None]).reshape(blocks * EDGE, cols)


def forward_kernel(tokens, gate, up, gate_mask, up_mask, gate_pre, up_pre):
    held = tokens[...]
    gate_pre[...] = dot(held, masked(gate[...], gate_mask[...]), 1, 0)
    up_pre[...] = dot(held, masked(up[...], up_mask[...]), 1, 0)


def middle_kernel(cot, down, down_mask, gate_pre, up_pre, hidden, grad_gate_pre, grad_up_pre):
    grad_hidden = dot(cot[...], masked(down[...], down_mask[...]), 1, 1)
    pre, up = gate_pre[...], up_pre[...]
    sigmoid = jax.nn.sigmoid(pre)
    silu = pre * sigmoid
    hidden[...] = (silu * up).astype(jnp.bfloat16)
    grad_gate_pre[...] = (grad_hidden * up * sigmoid * (1.0 + pre * (1.0 - sigmoid))).astype(
        jnp.bfloat16
    )
    grad_up_pre[...] = (grad_hidden * silu).astype(jnp.bfloat16)


def input_kernel(grad_gate_pre, grad_up_pre, gate, up, gate_mask, up_mask, out):
    total = dot(grad_gate_pre[...], masked(gate[...], gate_mask[...]), 1, 1)
    total += dot(grad_up_pre[...], masked(up[...], up_mask[...]), 1, 1)
    out[...] = total.astype(jnp.bfloat16)


def outer_kernel(left, right, mask, out):
    cols = right.shape[1]
    step = min(cols, 512)
    flipped = left[...].T
    for start in range(0, cols, step):
        part = pl.ds(start, step)
        product = dot(flipped, right[:, part], 1, 0).astype(jnp.bfloat16)
        out[:, part] = masked(product, mask[:, :, part])


def call(kernel, name, grid, ins, outs, flops, args):
    moved = sum(a.size * a.dtype.itemsize for a in args) + sum(
        s.size * s.dtype.itemsize for s, _ in outs
    )
    single = len(outs) == 1
    shapes = [s for s, _ in outs]
    specs = [b for _, b in outs]
    return pl.pallas_call(
        kernel,
        name=name,
        grid=(grid,),
        in_specs=ins,
        out_shape=shapes[0] if single else shapes,
        out_specs=specs[0] if single else specs,
        compiler_params=pltpu.CompilerParams(vmem_limit_bytes=VMEM),
        cost_estimate=pl.CostEstimate(flops=flops, bytes_accessed=moved, transcendentals=0),
    )(*args)


def whole_of(array):
    return pl.BlockSpec(array.shape, lambda i: (0,) * array.ndim)


def forward(tokens, gate, up, gate_mask, up_mask):
    rows, width = tokens.shape
    units = gate.shape[1]
    tile = min(256, units)
    weight = pl.BlockSpec((width, tile), lambda i: (0, i))
    mask = pl.BlockSpec((width // EDGE, SUB, tile), lambda i: (0, 0, i))
    out = (
        jax.ShapeDtypeStruct((rows, units), jnp.float32),
        pl.BlockSpec((rows, tile), lambda i: (0, i)),
    )
    return call(
        forward_kernel, "forward", units // tile,
        [whole_of(tokens), weight, weight, mask, mask], [out, out],
        4 * rows * width * units, (tokens, gate, up, gate_mask, up_mask),
    )


def middle(cot, down, down_mask, gate_pre, up_pre):
    rows, width = cot.shape
    units = down.shape[0]
    tile = min(256, units)
    columns = pl.BlockSpec((rows, tile), lambda i: (0, i))
    out = (jax.ShapeDtypeStruct((rows, units), jnp.bfloat16), columns)
    return call(
        middle_kernel, "middle", units // tile,
        [
            whole_of(cot),
            pl.BlockSpec((tile, width), lambda i: (i, 0)),
            pl.BlockSpec((tile // EDGE, SUB, width), lambda i: (i, 0, 0)),
            columns,
            columns,
        ],
        [out, out, out],
        2 * rows * width * units, (cot, down, down_mask, gate_pre, up_pre),
    )


def input_part(grad_gate_pre, grad_up_pre, gate, up, gate_mask, up_mask, part, parts):
    rows, units = grad_gate_pre.shape
    width = gate.shape[0] // parts
    tile = min(512, width)
    first = part * width // tile
    weight = pl.BlockSpec((tile, units), lambda i: (i + first, 0))
    mask = pl.BlockSpec((tile // EDGE, SUB, units), lambda i: (i + first, 0, 0))
    out = (
        jax.ShapeDtypeStruct((rows, width), jnp.bfloat16),
        pl.BlockSpec((rows, tile), lambda i: (0, i)),
    )
    return call(
        input_kernel, "input_part", width // tile,
        [whole_of(grad_gate_pre), whole_of(grad_up_pre), weight, weight, mask, mask], [out],
        4 * rows * width * units,
        (grad_gate_pre, grad_up_pre, gate, up, gate_mask, up_mask),
    )


def outer(left, right, mask, name):
    rows, height = left.shape
    cols = right.shape[1]
    tile = max(EDGE, min(height, 1024 * 1024 // cols))
    out = (
        jax.ShapeDtypeStruct((height, cols), jnp.bfloat16),
        pl.BlockSpec((tile, cols), lambda i: (i, 0)),
    )
    return call(
        outer_kernel, name, height // tile,
        [
            pl.BlockSpec((rows, tile), lambda i: (0, i)),
            whole_of(right),
            pl.BlockSpec((tile // EDGE, SUB, cols), lambda i: (i, 0, 0)),
        ],
        [out], 2 * rows * height * cols, (left, right, mask),
    )


def expand(keep):
    rows, cols = keep.shape
    wide = jnp.broadcast_to(
        keep.astype(jnp.bfloat16)[:, None, :, None], (rows, SUB, cols, EDGE)
    )
    return wide.reshape(rows, SUB, cols * EDGE)


def shifted(array, axis, by):
    peers = lax.axis_size(axis)
    pairs = [(i, i + by) for i in range(peers) if 0 <= i + by < peers]
    return lax.ppermute(array, axis, pairs)


def swap(array, axis, bit):
    return lax.ppermute(array, axis, [(i, i ^ bit) for i in range(lax.axis_size(axis))])


def select_rows(noised):
    slot = jnp.cumsum(noised) - 1
    return (
        (slot[None, :] == jnp.arange(CAP)[:, None]) & (noised[None, :] > 0)
    ).astype(jnp.bfloat16)


def side_by_side(own, other):
    first = lax.axis_index("row") == 0
    return jnp.concatenate(
        [jnp.where(first, own, other), jnp.where(first, other, own)], axis=-1
    )


def gather_pairs(own):
    half = own.shape[0] // 2
    top, bottom = own[:half], own[half:]
    top_x = swap(top, "row", 1)
    bottom_y = swap(bottom, "col", 2)
    top_wide = side_by_side(top, top_x)
    bottom_both = jnp.stack([bottom, bottom_y])
    top_y = swap(top_wide, "col", 2)
    bottom_x = swap(bottom_both, "row", 1)
    top_both = jnp.stack([top_wide, top_y])
    bottom_wide = side_by_side(bottom_both, bottom_x)
    top_core = swap(top_both, "col", 1)
    bottom_core = swap(bottom_wide, "col", 1)
    parts = [
        piece
        for y in range(2)
        for pair in ((top_both, bottom_wide), (top_core, bottom_core))
        for piece in (pair[0][y], pair[1][y])
    ]
    return jnp.concatenate(parts, axis=0)


def add(left, right):
    return (left.astype(jnp.float32) + right.astype(jnp.float32)).astype(jnp.bfloat16)


def by_row(block):
    half = block.shape[1] // 2
    first = lax.axis_index("row") == 0
    top, bottom = block[:, :half], block[:, half:]
    return jnp.where(first, top, bottom), jnp.where(first, bottom, top)


def scatter_pairs(left, right):
    def core(block):
        block = block.reshape(2, 2, CAP, block.shape[1])
        return add(block[:, 0], swap(block[:, 1], "col", 1))

    left, right = core(left), core(right)
    left = add(left[:1], swap(left[1:], "col", 2))
    keep, send = by_row(right)
    right = add(keep, swap(send, "row", 1))
    keep, send = by_row(left)
    left = add(keep, swap(send, "row", 1))[0]
    right = add(right[0], swap(right[1], "col", 2))
    return left, right


def on_device(tokens, cotangent, noised, gate_weight, up_weight, down_weight, block_keep):
    rows, cols = lax.axis_size("row"), lax.axis_size("col")
    paired = rows == 2 and cols == 4
    local_noised = noised[0]
    gate, up, down = gate_weight[0], up_weight[0], down_weight[0]
    gate_mask = expand(block_keep[0, 0])
    up_mask = expand(block_keep[0, 1])
    down_mask = expand(block_keep[0, 2].T)
    selector = select_rows(local_noised)
    next_selector = select_rows(shifted(local_noised, "section", -1))
    sent_tokens = dot(selector, tokens[0], 1, 0).astype(jnp.bfloat16)
    masked_cot = cotangent[0] * local_noised[:, None].astype(jnp.bfloat16)
    sent_cot = dot(selector, masked_cot, 1, 0).astype(jnp.bfloat16)

    def gather(block):
        wide = lax.all_gather(block, "row", axis=1, tiled=True)
        wide = wide.reshape(rows, CAP // rows, wide.shape[1])
        wide = lax.all_gather(wide, "col", axis=1, tiled=True)
        return wide.reshape(cols * CAP, wide.shape[2])

    if paired:
        all_tokens = gather_pairs(sent_tokens)
        sent_cot, _ = lax.optimization_barrier((sent_cot, all_tokens))
        all_cot = gather_pairs(sent_cot)
    else:
        all_tokens, all_cot = gather(sent_tokens), gather(sent_cot)
    gate_pre, up_pre = forward(all_tokens, gate, up, gate_mask, up_mask)
    hidden, grad_gate_pre, grad_up_pre = middle(all_cot, down, down_mask, gate_pre, up_pre)
    halves = [
        input_part(grad_gate_pre, grad_up_pre, gate, up, gate_mask, up_mask, part, 2)
        for part in range(2)
    ]
    grad_down = outer(hidden, all_cot, down_mask, "grad_down")
    grad_gate = outer(all_tokens, grad_gate_pre, gate_mask, "grad_gate")
    grad_up = outer(all_tokens, grad_up_pre, up_mask, "grad_up")
    if paired:
        pieces = [shifted(piece, "section", -1) for piece in scatter_pairs(*halves)]
        first = lax.axis_index("row") == 0
        blocks = []
        for piece in pieces:
            other = swap(piece, "row", 1)
            blocks.append(
                jnp.concatenate([jnp.where(first, piece, other), jnp.where(first, other, piece)])
            )
        block = jnp.concatenate(blocks, axis=1)
    else:
        share = lax.psum_scatter(
            jnp.concatenate(halves, axis=1).astype(jnp.float32),
            ("row", "col"),
            scatter_dimension=0,
            tiled=True,
        ).astype(jnp.bfloat16)
        share = shifted(share, "section", -1)
        block = lax.all_gather(share, "row", axis=0, tiled=True)
    handoff = dot(next_selector, block, 0, 0).astype(jnp.bfloat16)
    return (grad_gate[None], grad_up[None], grad_down[None], handoff[None])


def solution(mesh):
    placed = (
        P("section", "col", "row"),
        P("section", "col", "row"),
        P("section", "col"),
        P("section", None, ("row", "col")),
        P("section", None, ("row", "col")),
        P("section", ("row", "col"), None),
        P("section", None, None, ("row", "col")),
    )
    return jax.shard_map(
        on_device,
        mesh=mesh,
        in_specs=placed,
        out_specs=(
            P("section", None, ("row", "col")),
            P("section", None, ("row", "col")),
            P("section", ("row", "col"), None),
            P("section", "col", None),
        ),
        check_vma=False,
    )
```

```python
import jax
import jax.numpy as jnp
from jax import lax
from jax.experimental import pallas as pl
from jax.experimental.pallas import tpu as pltpu
from jax.sharding import PartitionSpec as P

CAP = 96
EDGE = 128
SUB = 16
VMEM = 44 * 1024 * 1024


def dot(left, right, left_dim, right_dim):
    return lax.dot_general(
        left,
        right,
        (((left_dim,), (right_dim,)), ((), ())),
        preferred_element_type=jnp.float32,
    )


def masked(values, mask):
    blocks, _, cols = mask.shape
    split = values.reshape(blocks, EDGE // SUB, SUB, cols)
    return (split * mask[:, None]).reshape(blocks * EDGE, cols)


def forward_kernel(tokens, weight, mask, out):
    out[...] = dot(tokens[...], masked(weight[...], mask[...]), 1, 0)


def middle_kernel(cot, down, down_mask, gate_pre, up_pre, hidden, grad_gate_pre, grad_up_pre):
    grad_hidden = dot(cot[...], masked(down[...], down_mask[...]), 1, 1)
    pre, up = gate_pre[...], up_pre[...]
    sigmoid = jax.nn.sigmoid(pre)
    silu = pre * sigmoid
    hidden[...] = (silu * up).astype(jnp.bfloat16)
    grad_gate_pre[...] = (grad_hidden * up * sigmoid * (1.0 + pre * (1.0 - sigmoid))).astype(
        jnp.bfloat16
    )
    grad_up_pre[...] = (grad_hidden * silu).astype(jnp.bfloat16)


def input_kernel(grad_gate_pre, grad_up_pre, gate, up, gate_mask, up_mask, out):
    total = dot(grad_gate_pre[...], masked(gate[...], gate_mask[...]), 1, 1)
    total += dot(grad_up_pre[...], masked(up[...], up_mask[...]), 1, 1)
    out[...] = total.astype(jnp.bfloat16)


def outer_kernel(left, right, mask, out, flag):
    flag[...] = jnp.zeros_like(flag)
    cols = right.shape[1]
    step = min(cols, 512)
    flipped = left[...].T
    for start in range(0, cols, step):
        part = pl.ds(start, step)
        product = dot(flipped, right[:, part], 1, 0).astype(jnp.bfloat16)
        out[:, part] = masked(product, mask[:, :, part])


def call(kernel, name, grid, ins, outs, flops, args, behind=(), into=None):
    moved = sum(a.size * a.dtype.itemsize for a in args) + sum(
        s.size * s.dtype.itemsize for s, _ in outs
    )
    single = len(outs) == 1
    shapes = [s for s, _ in outs]
    specs = [b for _, b in outs]
    used = len(args)
    others = ([] if into is None else [into]) + list(behind)

    def body(*refs):
        kernel(*refs[:used], *refs[used + len(others):])

    return pl.pallas_call(
        body,
        name=name,
        grid=(grid,),
        in_specs=ins + [pl.BlockSpec(memory_space=pl.ANY)] * len(others),
        input_output_aliases={} if into is None else {used: 0},
        out_shape=shapes[0] if single else shapes,
        out_specs=specs[0] if single else specs,
        compiler_params=pltpu.CompilerParams(vmem_limit_bytes=VMEM),
        cost_estimate=pl.CostEstimate(flops=flops, bytes_accessed=moved, transcendentals=0),
    )(*args, *others)


def whole_of(array):
    return pl.BlockSpec(array.shape, lambda i: (0,) * array.ndim)


def forward(tokens, weight, mask, name, behind=()):
    rows, width = tokens.shape
    units = weight.shape[1]
    tile = min(256, units)
    out = (
        jax.ShapeDtypeStruct((rows, units), jnp.float32),
        pl.BlockSpec((rows, tile), lambda i: (0, i)),
    )
    return call(
        forward_kernel, name, units // tile,
        [
            whole_of(tokens),
            pl.BlockSpec((width, tile), lambda i: (0, i)),
            pl.BlockSpec((width // EDGE, SUB, tile), lambda i: (0, 0, i)),
        ],
        [out], 2 * rows * width * units, (tokens, weight, mask), behind,
    )


def middle(cot, down, down_mask, gate_pre, up_pre):
    rows, width = cot.shape
    units = down.shape[0]
    tile = min(256, units)
    columns = pl.BlockSpec((rows, tile), lambda i: (0, i))
    out = (jax.ShapeDtypeStruct((rows, units), jnp.bfloat16), columns)
    return call(
        middle_kernel, "middle", units // tile,
        [
            whole_of(cot),
            pl.BlockSpec((tile, width), lambda i: (i, 0)),
            pl.BlockSpec((tile // EDGE, SUB, width), lambda i: (i, 0, 0)),
            columns,
            columns,
        ],
        [out, out, out],
        2 * rows * width * units, (cot, down, down_mask, gate_pre, up_pre),
    )


def input_part(grad_gate_pre, grad_up_pre, gate, up, gate_mask, up_mask, part, parts, behind=()):
    rows, units = grad_gate_pre.shape
    width = gate.shape[0] // parts
    tile = min(512, width)
    first = part * width // tile
    weight = pl.BlockSpec((tile, units), lambda i: (i + first, 0))
    mask = pl.BlockSpec((tile // EDGE, SUB, units), lambda i: (i + first, 0, 0))
    out = (
        jax.ShapeDtypeStruct((rows, width), jnp.bfloat16),
        pl.BlockSpec((rows, tile), lambda i: (0, i)),
    )
    return call(
        input_kernel, "input_part", width // tile,
        [whole_of(grad_gate_pre), whole_of(grad_up_pre), weight, weight, mask, mask], [out],
        4 * rows * width * units,
        (grad_gate_pre, grad_up_pre, gate, up, gate_mask, up_mask), behind,
    )


def outer(left, right, mask, name, part=0, parts=1, behind=(), into=None):
    rows, height = left.shape
    cols = right.shape[1]
    tile = max(EDGE, min(height // parts, 1024 * 1024 // cols))
    count = height // parts // tile
    first = part * count
    out = (
        jax.ShapeDtypeStruct((height, cols), jnp.bfloat16),
        pl.BlockSpec((tile, cols), lambda i: (i + first, 0)),
    )
    flag = (
        jax.ShapeDtypeStruct((8, EDGE), jnp.float32),
        pl.BlockSpec((8, EDGE), lambda i: (0, 0)),
    )
    return call(
        outer_kernel, name, count,
        [
            pl.BlockSpec((rows, tile), lambda i: (0, i + first)),
            whole_of(right),
            pl.BlockSpec((tile // EDGE, SUB, cols), lambda i: (i + first, 0, 0)),
        ],
        [out, flag], 2 * rows * height * cols // parts, (left, right, mask), behind, into,
    )


def expand(keep):
    rows, cols = keep.shape
    wide = jnp.broadcast_to(
        keep.astype(jnp.bfloat16)[:, None, :, None], (rows, SUB, cols, EDGE)
    )
    return wide.reshape(rows, SUB, cols * EDGE)


def shifted(array, axis, by):
    peers = lax.axis_size(axis)
    pairs = [(i, i + by) for i in range(peers) if 0 <= i + by < peers]
    return lax.ppermute(array, axis, pairs)


def swap(array, axis, bit):
    return lax.ppermute(array, axis, [(i, i ^ bit) for i in range(lax.axis_size(axis))])


def select_rows(noised):
    slot = jnp.cumsum(noised) - 1
    return (
        (slot[None, :] == jnp.arange(CAP)[:, None]) & (noised[None, :] > 0)
    ).astype(jnp.bfloat16)


def side_by_side(own, other):
    first = lax.axis_index("row") == 0
    return jnp.concatenate(
        [jnp.where(first, own, other), jnp.where(first, other, own)], axis=-1
    )


def gather_near(top, bottom):
    return swap(top, "row", 1), swap(bottom, "col", 2)


def gather_wide(top, bottom, top_x, bottom_y):
    return side_by_side(top, top_x), jnp.stack([bottom, bottom_y])


def gather_far(top_wide, bottom_both):
    return swap(top_wide, "col", 2), swap(bottom_both, "row", 1)


def gather_chip(top_wide, bottom_both, top_y, bottom_x):
    return jnp.concatenate(
        [jnp.stack([top_wide, top_y]), side_by_side(bottom_both, bottom_x)], axis=1
    )


def gather_all(own):
    other = swap(own, "col", 1)
    return jnp.concatenate([own[0], other[0], own[1], other[1]], axis=0)


def add(left, right):
    return (left.astype(jnp.float32) + right.astype(jnp.float32)).astype(jnp.bfloat16)


def by_row(block):
    half = block.shape[1] // 2
    first = lax.axis_index("row") == 0
    top, bottom = block[:, :half], block[:, half:]
    return jnp.where(first, top, bottom), jnp.where(first, bottom, top)


def both_rows(piece, other):
    first = lax.axis_index("row") == 0
    return jnp.concatenate([jnp.where(first, piece, other), jnp.where(first, other, piece)])


def after(array, *others):
    return lax.optimization_barrier((array, *others))[0]


def paired_device(tokens, cotangent, noised, gate, up, down, keep):
    selector = select_rows(noised)
    half = CAP // 2
    rows_of = (selector[:half], selector[half:])
    t_top, t_bottom = (dot(r, tokens, 1, 0).astype(jnp.bfloat16) for r in rows_of)
    t_near = gather_near(t_top, t_bottom)
    c_top, c_bottom = (
        dot(after(r, t_top, t_bottom), cotangent, 1, 0).astype(jnp.bfloat16) for r in rows_of
    )
    gate_keep, up_keep, down_keep = lax.optimization_barrier((*keep, t_top, t_bottom))[:3]
    gate_mask, up_mask, down_mask = expand(gate_keep), expand(up_keep), expand(down_keep.T)
    t_wide = gather_wide(t_top, t_bottom, *t_near)
    t_far = gather_far(*t_wide)
    t_chip = gather_chip(*t_wide, *t_far)
    c_top, c_bottom, _ = lax.optimization_barrier((c_top, c_bottom, t_chip))
    c_near = gather_near(c_top, c_bottom)
    all_tokens = gather_all(t_chip)
    c_wide = gather_wide(c_top, c_bottom, *c_near)
    c_far = gather_far(*c_wide)
    gate_pre = forward(all_tokens, gate, gate_mask, "gate_pre", c_wide)
    c_chip = gather_chip(*c_wide, *c_far)
    c_chip = after(c_chip, gate_pre)
    up_pre = forward(all_tokens, up, up_mask, "up_pre", (c_chip,))
    all_cot = gather_all(c_chip)
    hidden, d_gate, d_up = middle(all_cot, down, down_mask, gate_pre, up_pre)
    next_selector = select_rows(shifted(after(noised, gate_pre), "section", -1))

    def core_split(block):
        block = block.reshape(2, 2, CAP, block.shape[1])
        return block[:, 0], block[:, 1]

    left = input_part(d_gate, d_up, gate, up, gate_mask, up_mask, 0, 2)
    l_keep, l_send = core_split(left)
    l_got = swap(l_send, "col", 1)
    right = input_part(d_gate, d_up, gate, up, gate_mask, up_mask, 1, 2, (l_send,))

    l_sum = add(l_keep, after(l_got, right))
    r_keep, r_send = core_split(right)
    l_got, r_got = swap(l_sum[1], "col", 2), swap(r_send, "col", 1)
    grad_down, done = outer(hidden, all_cot, down_mask, "grad_down", 0, 1, (l_sum, r_send))

    l_keep, l_send = by_row(add(l_sum[:1], after(l_got, done)[None]))
    r_keep, r_send = by_row(add(r_keep, after(r_got, done)))
    l_got, r_got = swap(l_send, "row", 1), swap(r_send, "row", 1)
    grad_up, done = outer(all_tokens, d_up, up_mask, "grad_up_a", 0, 2, (l_send, r_send))

    l_own = add(l_keep, after(l_got, done))[0]
    r_sum = add(r_keep, after(r_got, done))
    l_got, r_got = shifted(l_own, "section", -1), swap(r_sum[1], "col", 2)
    grad_up, done = outer(all_tokens, d_up, up_mask, "grad_up_b", 1, 2, (l_own, r_sum), grad_up)

    l_piece = after(l_got, done)
    r_own = add(r_sum[0], after(r_got, done))
    l_got, r_got = swap(l_piece, "row", 1), shifted(r_own, "section", -1)
    grad_gate, done = outer(all_tokens, d_gate, gate_mask, "grad_gate_a", 0, 2, (l_piece, r_own))

    l_block = both_rows(l_piece, after(l_got, done))
    r_piece = after(r_got, done)
    r_got = swap(r_piece, "row", 1)
    grad_gate, done = outer(
        all_tokens, d_gate, gate_mask, "grad_gate_b", 1, 2, (l_block, r_piece), grad_gate
    )
    block = jnp.concatenate([l_block, both_rows(r_piece, after(r_got, done))], axis=1)
    handoff = dot(next_selector, block, 0, 0).astype(jnp.bfloat16)
    return grad_gate[None], grad_up[None], grad_down[None], handoff[None]


def on_device(tokens, cotangent, noised, gate_weight, up_weight, down_weight, block_keep):
    rows, cols = lax.axis_size("row"), lax.axis_size("col")
    local_noised = noised[0]
    gate, up, down = gate_weight[0], up_weight[0], down_weight[0]
    masked_cot = cotangent[0] * local_noised[:, None].astype(jnp.bfloat16)
    if rows == 2 and cols == 4:
        keep = tuple(block_keep[0, i] for i in range(3))
        return paired_device(tokens[0], masked_cot, local_noised, gate, up, down, keep)
    gate_mask = expand(block_keep[0, 0])
    up_mask = expand(block_keep[0, 1])
    down_mask = expand(block_keep[0, 2].T)
    selector = select_rows(local_noised)
    next_selector = select_rows(shifted(local_noised, "section", -1))
    sent_tokens = dot(selector, tokens[0], 1, 0).astype(jnp.bfloat16)
    sent_cot = dot(selector, masked_cot, 1, 0).astype(jnp.bfloat16)

    def gather(block):
        wide = lax.all_gather(block, "row", axis=1, tiled=True)
        wide = wide.reshape(rows, CAP // rows, wide.shape[1])
        wide = lax.all_gather(wide, "col", axis=1, tiled=True)
        return wide.reshape(cols * CAP, wide.shape[2])

    all_tokens, all_cot = gather(sent_tokens), gather(sent_cot)
    gate_pre = forward(all_tokens, gate, gate_mask, "gate_pre")
    up_pre = forward(all_tokens, up, up_mask, "up_pre")
    hidden, grad_gate_pre, grad_up_pre = middle(all_cot, down, down_mask, gate_pre, up_pre)
    halves = [
        input_part(grad_gate_pre, grad_up_pre, gate, up, gate_mask, up_mask, part, 2)
        for part in range(2)
    ]
    grad_down = outer(hidden, all_cot, down_mask, "grad_down")[0]
    grad_gate = outer(all_tokens, grad_gate_pre, gate_mask, "grad_gate")[0]
    grad_up = outer(all_tokens, grad_up_pre, up_mask, "grad_up")[0]
    share = lax.psum_scatter(
        jnp.concatenate(halves, axis=1).astype(jnp.float32),
        ("row", "col"),
        scatter_dimension=0,
        tiled=True,
    ).astype(jnp.bfloat16)
    share = shifted(share, "section", -1)
    block = lax.all_gather(share, "row", axis=0, tiled=True)
    handoff = dot(next_selector, block, 0, 0).astype(jnp.bfloat16)
    return (grad_gate[None], grad_up[None], grad_down[None], handoff[None])


def solution(mesh):
    placed = (
        P("section", "col", "row"),
        P("section", "col", "row"),
        P("section", "col"),
        P("section", None, ("row", "col")),
        P("section", None, ("row", "col")),
        P("section", ("row", "col"), None),
        P("section", None, None, ("row", "col")),
    )
    return jax.shard_map(
        on_device,
        mesh=mesh,
        in_specs=placed,
        out_specs=(
            P("section", None, ("row", "col")),
            P("section", None, ("row", "col")),
            P("section", ("row", "col"), None),
            P("section", "col", None),
        ),
        check_vma=False,
    )
```
